32 devices in a mesh: replica: 16 (over z, y, core), shard: 2 (over x).
Axes of the slice: x: 2, y: 2, z: 4, core: 2. Of those that a mesh axis runs over, the one named last changes fastest.
Arguments:
- tokens: bfloat16 [8192, 768], P(('replica', 'shard')), may hold values from -6 to 6
- cotangent: bfloat16 [8192, 768], P(('replica', 'shard')), may hold values from -6 to 6
- positions: int32 [8192], P(('replica', 'shard')), may hold values from 0 to 1023, as said below
- rest: int32 [8192], P(('replica', 'shard')), may hold values from 0 to 1023, as said below
- first_gain: bfloat16 [768], P('shard'), may hold values from 0.25 to 1.75
- second_gain: bfloat16 [768], P('shard'), may hold values from 0.25 to 1.75
- merged_weight: bfloat16 [768, 2304], P('shard'), may hold values from -0.21875 to 0.21875
- output_weight: bfloat16 [768, 768], P('shard'), may hold values from -0.875 to 0.875
- input_weight: bfloat16 [768, 2304], P('shard'), may hold values from -0.21875 to 0.21875
- down_weight: bfloat16 [1152, 768], P('shard'), may hold values from -0.1875 to 0.1875
Outputs:
- mixed: bfloat16 [8192, 768], P(('replica', 'shard'))
- token_grad: float32 [8192, 768], P(('replica', 'shard'))
- first_gain_grad: float32 [768], P('shard')
- second_gain_grad: float32 [768], P('shard')
- merged_grad: float32 [768, 2304], P('shard')
- output_grad: float32 [768, 768], P('shard')
- input_grad: float32 [768, 2304], P('shard')
- down_grad: float32 [1152, 768], P('shard')
The draws below stay inside these ranges and needn't reach their ends.
Inputs may be any that keep to these rules, and one draw needn't show every extreme that they name: Documents are packed end to end, the first entered part way: positions[t + 1] = positions[t] + 1 and rest[t + 1] = rest[t] - 1 inside a document, and where rest[t] = 0 the next token starts a new document with position 0. Every document has 512 to 1024 tokens (the first and last may be cut by the ends), and one has exactly 1024. rest[t] + positions[t] + 1 is the length of t's document.
All inputs are finite; a program needn't handle non-finite values.
Results may differ from the reference program's by a relative error of at most 0.024.
Values may be sent and summed in bfloat16 or wider, within the bound.
A program may use at most 128 MiB of HBM per device.

```python
import math
import jax
import jax.numpy as jnp
from jax import lax

D = 768
HEADS = 12
HEAD_DIM = 64
FF = 1152
WINDOW = 64
SEQ = 1024
TOKENS = 8192


def document_layout(key):
    count = TOKENS // (SEQ // 2) + 3
    lengths = jax.random.randint(key, (count,), SEQ // 2, SEQ + 1).astype(jnp.int32)
    lengths = lengths.at[1].set(SEQ)
    skip = jax.random.randint(jax.random.fold_in(key, 11), (), 0, lengths[0]).astype(jnp.int32)
    ends = jnp.cumsum(lengths).astype(jnp.int32) - skip
    starts = ends - lengths
    index = jnp.arange(TOKENS, dtype=jnp.int32)
    which = jnp.sum((ends[None, :] <= index[:, None]).astype(jnp.int32), 1).astype(jnp.int32)
    first = jnp.take(starts, which)
    last = jnp.take(ends, which)
    place = jnp.maximum(index - first, 0).astype(jnp.int32)
    after = (last - 1 - index).astype(jnp.int32)
    return (place, after)


def draw_positions(key, part):
    place, after = document_layout(key)
    return place


def draw_rest(key, part):
    place, after = document_layout(key)
    return after


def steps_of(stream_key, dims, shards, low, high):
    def one(position, shards_of):
        steps = jax.random.uniform(jax.random.fold_in(jax.random.fold_in(stream_key, 6), position), (shards_of,), jnp.float32, low / len(shards), high / len(shards))
        return jnp.repeat(jnp.exp(steps), dims[position] // shards_of).reshape((-1,) + (1,) * (len(dims) - position - 1))

    factor_of = one(*shards[0])
    for cut in shards[1:]:
        factor_of = factor_of * one(*cut)
    return factor_of


def gaussian(stream_key, extent, deviation, most, pieces=(), kind=jnp.bfloat16):
    values = deviation * jax.random.normal(stream_key, extent, jnp.float32)
    if pieces:
        values = values * steps_of(stream_key, extent, pieces, -0.22, 0.18)
    return jnp.clip(values, -most, most).astype(kind)


def setup_inputs(seed: int = 0) -> dict:
    streams_of = jax.random.split(jax.random.key(seed), 11)
    tokens = gaussian(streams_of[0], (TOKENS, D), 1.0, 6.0, ((0, 32),))
    cotangent = gaussian(streams_of[1], (TOKENS, D), 1.0, 6.0, ((0, 32),))
    positions = draw_positions(jax.random.fold_in(streams_of[10], 71), 0)
    rest = draw_rest(jax.random.fold_in(streams_of[10], 71), 0)
    first_gain = jnp.clip(1.0 + 0.15 * jax.random.normal(streams_of[4], (D,), jnp.float32), 0.25, 1.75).astype(jnp.bfloat16)
    second_gain = jnp.clip(1.0 + 0.15 * jax.random.normal(streams_of[5], (D,), jnp.float32), 0.25, 1.75).astype(jnp.bfloat16)
    merged_weight = gaussian(streams_of[6], (D, 3 * D), D ** -0.5, 0.21875, ((0, 2),))
    output_weight = gaussian(streams_of[7], (D, D), (D // 16) ** -0.5, 0.875, ((0, 2),))
    input_weight = gaussian(streams_of[8], (D, 2 * FF), D ** -0.5, 0.21875, ((0, 2),))
    down_weight = gaussian(streams_of[9], (FF, D), FF ** -0.5, 0.1875, ((0, 2),))
    return dict(tokens=tokens, cotangent=cotangent, positions=positions, rest=rest, first_gain=first_gain, second_gain=second_gain, merged_weight=merged_weight, output_weight=output_weight, input_weight=input_weight, down_weight=down_weight)


@jax.custom_vjp
def low(v):
    return lax.optimization_barrier(v.astype(jnp.bfloat16)).astype(jnp.float32)

@jax.custom_vjp
def low_back(v):
    return v

def low_keep(v):
    return (low(v), None)

def low_pass(kept, grad):
    return (grad,)

def back_keep(v):
    return (v, None)

def back_low(kept, grad):
    return (low(grad),)
low.defvjp(low_keep, low_pass)
low_back.defvjp(back_keep, back_low)
EPSILON = 1e-05
NEGATIVE = -1e+30

def layer_norm(values, gain):
    centre = values - lax.optimization_barrier(jnp.mean(values, -1, keepdims=True))
    spread = lax.optimization_barrier(jnp.mean(centre * centre, -1, keepdims=True))
    return centre * lax.rsqrt(spread + EPSILON) * gain

def rotary_tables(positions):
    half = HEAD_DIM // 2
    freqs = jnp.exp(jnp.arange(half, dtype=jnp.float32) * (-2.0 * math.log(10000.0) / HEAD_DIM))
    angles = positions.astype(jnp.float32)[:, None] * freqs[None, :]
    angles = jnp.concatenate([angles, angles], -1)[:, None, :]
    return (jnp.cos(angles), jnp.sin(angles))

def rotate(values, cosine, sine):
    half = values.shape[-1] // 2
    turned = jnp.concatenate([-values[..., half:], values[..., :half]], -1)
    return values * cosine + turned * sine

def attend(query, keys, values, positions, rest):
    block_rows = 512
    scale = HEAD_DIM ** (-0.5)
    edges = ((WINDOW, WINDOW), (0, 0), (0, 0))
    keys_pad = jnp.pad(keys, edges)
    values_pad = jnp.pad(values, edges)
    starts = jnp.arange(TOKENS // block_rows, dtype=jnp.int32) * block_rows

    def one_block(start):
        start = start.astype(jnp.int32)
        query_block = lax.dynamic_slice_in_dim(query, start, block_rows, 0)
        keys_block = lax.dynamic_slice_in_dim(keys_pad, start, block_rows + 2 * WINDOW, 0)
        values_block = lax.dynamic_slice_in_dim(values_pad, start, block_rows + 2 * WINDOW, 0)
        place = lax.dynamic_slice_in_dim(positions, start, block_rows, 0)
        after = lax.dynamic_slice_in_dim(rest, start, block_rows, 0)
        rows = start + jnp.arange(block_rows, dtype=jnp.int32)
        cols = start - WINDOW + jnp.arange(block_rows + 2 * WINDOW, dtype=jnp.int32)
        offset = cols[None, :] - rows[:, None]
        allowed = (jnp.abs(offset) <= WINDOW) & (cols[None, :] >= 0) & (cols[None, :] < TOKENS)
        allowed = allowed & (-offset <= place[:, None]) & (offset <= after[:, None])
        scores = jnp.einsum('qhd,khd->hqk', query_block, keys_block, precision=lax.Precision.HIGHEST) * scale
        scores = low_back(scores)
        scores = jnp.where(allowed[None], scores, NEGATIVE)
        peak = lax.optimization_barrier(jnp.max(scores, -1, keepdims=True))
        expo = jnp.exp(scores - peak)
        prob = expo / lax.optimization_barrier(jnp.sum(expo, -1, keepdims=True))
        return jnp.einsum('hqk,khd->qhd', low(prob), values_block, precision=lax.Precision.HIGHEST)
    outputs = lax.map(jax.checkpoint(one_block), starts)
    return outputs.reshape(TOKENS, HEADS, HEAD_DIM)

def reference(tokens, cotangent, positions, rest, first_gain, second_gain, merged_weight, output_weight, input_weight, down_weight):
    highest = lax.Precision.HIGHEST
    cosine, sine = rotary_tables(positions)

    def forward(tokens_f, gain_one, gain_two, merged_w, output_w, input_w, down_w):
        norm_one = low(layer_norm(tokens_f, gain_one))
        merged = low_back(jnp.dot(norm_one, merged_w, precision=highest))
        query = merged[:, :D].reshape(TOKENS, HEADS, HEAD_DIM)
        keys = merged[:, D:2 * D].reshape(TOKENS, HEADS, HEAD_DIM)
        values = merged[:, 2 * D:].reshape(TOKENS, HEADS, HEAD_DIM)
        query = low(rotate(query, cosine, sine))
        keys = low(rotate(keys, cosine, sine))
        values = low(values)
        context = attend(query, keys, values, positions, rest).reshape(TOKENS, D)
        context = low(low_back(context))
        resid = tokens_f + low_back(jnp.dot(context, output_w, precision=highest))
        norm_two = low(layer_norm(resid, gain_two))
        hidden = low_back(jnp.dot(norm_two, input_w, precision=highest))
        act = low(jax.nn.gelu(hidden[:, :FF], approximate=False) * hidden[:, FF:])
        return resid + low_back(jnp.dot(act, down_w, precision=highest))
    inputs = tuple((a.astype(jnp.float32) for a in (tokens, first_gain, second_gain, merged_weight, output_weight, input_weight, down_weight)))
    mixed, pullback = jax.vjp(forward, *inputs)
    grads = pullback(cotangent.astype(jnp.float32))
    return (mixed.astype(jnp.bfloat16), grads[0], grads[1], grads[2], grads[3], grads[4], grads[5], grads[6])
```

```python
import functools
import math

import jax
import jax.numpy as jnp
from jax import lax
from jax.experimental import pallas as pl
from jax.experimental.pallas import tpu as pltpu
from jax.sharding import PartitionSpec as P

D = 768
HEADS = 12
HEAD_DIM = 64
FF = 1152
WINDOW = 64


EPSILON = 1e-05
NEGATIVE = -1e30


def extended(cells, sides, width):
    for axis, dim in sides:
        count = lax.axis_size(axis)
        ends = count - 1
        head = lax.slice_in_dim(cells, 0, width, axis=dim)
        tail = lax.slice_in_dim(cells, cells.shape[dim] - width, cells.shape[dim], axis=dim)
        cells = jnp.concatenate(
            [
                lax.ppermute(tail, axis, [(i, (i + 1) % count) for i in range(ends)]),
                cells,
                lax.ppermute(head, axis, [((i + 1) % count, i) for i in range(ends)]),
            ],
            axis=dim,
        )
    return cells


def layer_norm(values, gain):
    centre = values - jnp.mean(values, -1, keepdims=True)
    spread = jnp.mean(centre * centre, -1, keepdims=True)
    return centre * lax.rsqrt(spread + EPSILON) * gain


def rotary_tables(positions):
    half = HEAD_DIM // 2
    freqs = jnp.exp(jnp.arange(half, dtype=jnp.float32) * (-2.0 * math.log(10000.0) / HEAD_DIM))
    angles = positions.astype(jnp.float32)[:, None] * freqs[None, :]
    angles = jnp.concatenate([angles, angles], -1)[:, None, :]
    return (jnp.cos(angles), jnp.sin(angles))


def rotate(values, cosine, sine):
    half = values.shape[-1] // 2
    turned = jnp.concatenate([-values[..., half:], values[..., :half]], -1)
    return values * cosine + turned * sine


def unrotate(grads, cosine, sine):
    pull = jax.vjp(lambda inner: rotate(inner, cosine, sine), grads)[1]
    return pull(grads)[0]


def gated(gate, up):
    return jax.nn.gelu(gate, approximate=False) * up


def window_mask(positions, rest, rows, place, count):
    query_rows = jnp.arange(rows, dtype=jnp.int32)[:, None]
    key_cols = jnp.arange(rows + 2 * WINDOW, dtype=jnp.int32)[None, :]
    offset = key_cols - WINDOW - query_rows
    allowed = (
        (jnp.abs(offset) <= WINDOW) & (-offset <= positions[:, None]) & (offset <= rest[:, None])
    )
    allowed = allowed & ((key_cols >= WINDOW) | (place > 0))
    allowed = allowed & ((key_cols < rows + WINDOW) | (place < count - 1))
    return allowed


PACK = 768
UNIT = 16
MESH = pl.DeviceIdType.MESH


def greet(peers):
    barrier = pltpu.get_barrier_semaphore()
    for peer in peers:
        pl.semaphore_signal(barrier, inc=1, device_id=peer, device_id_type=MESH)
    pl.semaphore_wait(barrier, len(peers))


def gather_kernel(shards, splits, *refs):
    count = len(splits)
    sources, fulls = refs[:count], refs[count : 2 * count]
    send_sem, recv_sem = refs[2 * count :]
    replica = lax.axis_index("replica")
    me = lax.axis_index("shard")
    core = lax.rem(replica, 2)
    side = lax.rem(lax.div(replica, 2), 2)
    core_peer = (replica + 1 - 2 * core, me)
    side_peer = (replica + 2 - 4 * side, me)
    greet(
        [(replica, lax.rem(me + off, shards)) for off in range(1, shards)] + [core_peer, side_peer]
    )

    def part(which, row_half, col_half):
        rows, cols = sources[which].shape
        by_rows, by_cols = splits[which]
        take_rows, take_cols = pl.ds(0, rows), pl.ds(0, cols)
        if by_rows:
            take_rows = pl.ds(pl.multiple_of(row_half * (rows // 2), UNIT), rows // 2)
        if by_cols:
            take_cols = pl.ds(pl.multiple_of(col_half * (cols // 2), 128), cols // 2)
        return take_rows, take_cols

    def copy(which, off, kind, source, target, peer):
        return pltpu.make_async_remote_copy(
            src_ref=source,
            dst_ref=target,
            send_sem=send_sem.at[which, off - 1, kind],
            recv_sem=recv_sem.at[which, off - 1, kind],
            device_id=peer,
            device_id_type=MESH,
        )

    def place(which, owner, row_half, col_half):
        return fulls[which].at[(owner,) + part(which, row_half, col_half)]

    copies = {}
    for which in range(count):
        for off in range(1, shards):
            copies[which, off, 0] = copy(
                which,
                off,
                0,
                sources[which].at[part(which, side, core)],
                place(which, me, side, core),
                (replica, lax.rem(me + off, shards)),
            )
            copies[which, off, 0].start()
    for which in range(count):
        fulls[which][me] = sources[which][...]

    def forward(which):
        by_rows, by_cols = splits[which]
        for off in range(1, shards):
            owner = lax.rem(me + shards - off, shards)
            piece = place(which, owner, side, core)
            copies[which, off, 0].wait_recv()
            if by_rows:
                copies[which, off, 1] = copy(which, off, 1, piece, piece, side_peer)
                copies[which, off, 1].start()
            if by_cols:
                copies[which, off, 2] = copy(which, off, 2, piece, piece, core_peer)
                copies[which, off, 2].start()

    def cross(which):
        by_rows, by_cols = splits[which]
        for off in range(1, shards):
            owner = lax.rem(me + shards - off, shards)
            if by_rows:
                copies[which, off, 1].wait_recv()
                if by_cols:
                    piece = place(which, owner, 1 - side, core)
                    copies[which, off, 3] = copy(which, off, 3, piece, piece, core_peer)
                    copies[which, off, 3].start()

    for which in range(count + 1):
        if which < count:
            forward(which)
        if which > 0:
            cross(which - 1)
    for which in range(count):
        for off in range(1, shards):
            for kind in (2, 3):
                if (which, off, kind) in copies:
                    copies[which, off, kind].wait_recv()
    for one in copies.values():
        one.wait_send()


def gather_weights(weights, shards):
    splits = tuple(
        (w.shape[0] % (2 * UNIT) == 0, w.shape[1] % 256 == 0 and w.shape[0] > UNIT)
        for w in weights
    )
    count = len(weights)
    fulls = pl.pallas_call(
        functools.partial(gather_kernel, shards, splits),
        out_shape=[jax.ShapeDtypeStruct((shards,) + w.shape, w.dtype) for w in weights],
        in_specs=[pl.BlockSpec(memory_space=pltpu.VMEM)] * count,
        out_specs=[pl.BlockSpec(memory_space=pltpu.VMEM)] * count,
        scratch_shapes=[
            pltpu.SemaphoreType.DMA((count, shards - 1, 4)),
            pltpu.SemaphoreType.DMA((count, shards - 1, 4)),
        ],
        compiler_params=pltpu.CompilerParams(
            collective_id=0, has_side_effects=True, vmem_limit_bytes=40 * 1024 * 1024
        ),
        name="gather_weights",
    )(*weights)
    return fulls


def reduce_kernel(shards, depth, chunks, rows, count, *refs):
    matrices, total = refs[:count], refs[count]
    terms, core_in, shard_in, side_in, deep_in, packs, sends, recvs = refs[count + 1 :]
    loads, filled = [], 0
    for matrix in matrices:
        taken = matrix.shape[1]
        for left in range(0, matrix.shape[2], PACK):
            load = pltpu.make_async_copy(
                matrix.at[:, :, pl.ds(left, PACK)],
                terms.at[:, pl.ds(filled, taken), :],
                packs.at[len(loads)],
            )
            load.start()
            loads.append(load)
            filled += taken
    if filled < chunks * rows:
        terms[:, filled:, :] = jnp.zeros((shards, chunks * rows - filled, PACK), terms.dtype)
    replica = lax.axis_index("replica")
    me = lax.axis_index("shard")
    core = lax.rem(replica, 2)
    side = lax.rem(lax.div(replica, 2), 2)
    level = lax.div(replica, 4)
    half, quarter, leaf = rows // 2, rows // 4, rows // (4 * depth)
    core_peer = (replica + 1 - 2 * core, me)
    side_peer = (replica + 2 - 4 * side, me)
    shard_peers = [(replica, lax.rem(me + off, shards)) for off in range(1, shards)]
    levels = [lax.rem(level + off, depth) for off in range(1, depth)]
    deep_peers = [(4 * other + lax.rem(replica, 4), me) for other in levels]
    greet([core_peer, side_peer] + shard_peers + deep_peers)
    for load in loads:
        load.wait()
    first_shard, first_side, first_deep = 1, shards, shards + 1
    back_deep, back_side, back_core = shards + depth, shards + 2 * depth - 1, shards + 2 * depth

    def copy(chunk, slot, source, target, peer):
        return pltpu.make_async_remote_copy(
            src_ref=source,
            dst_ref=target,
            send_sem=sends.at[chunk, slot],
            recv_sem=recvs.at[chunk, slot],
            device_id=peer,
            device_id_type=MESH,
        )

    def span(start, size):
        return pl.ds(pl.multiple_of(start, UNIT), size)

    def wide(cells):
        return cells.astype(jnp.float32)

    def to_core(k):
        source = terms.at[:, span(k * rows + (1 - core) * half, half), :]
        return [copy(k, 0, source, core_in.at[k], core_peer)]

    def to_shard(k):
        return [
            copy(
                k,
                first_shard + i,
                core_in.at[k, lax.rem(me + i + 1, shards)],
                shard_in.at[k, i],
                shard_peers[i],
            )
            for i in range(shards - 1)
        ]

    def to_side(k):
        source = core_in.at[k, me, span((1 - side) * quarter, quarter), :]
        return [copy(k, first_side, source, side_in.at[k], side_peer)]

    def to_deep(k):
        return [
            copy(
                k,
                first_deep + i,
                side_in.at[k, span(levels[i] * leaf, leaf), :],
                deep_in.at[k, i],
                deep_peers[i],
            )
            for i in range(depth - 1)
        ]

    def same(k, slot, start, size, peer):
        region = total.at[span(k * rows + start, size), :]
        return copy(k, slot, region, region, peer)

    def from_deep(k):
        start = core * half + side * quarter + level * leaf
        return [same(k, back_deep + i, start, leaf, deep_peers[i]) for i in range(depth - 1)]

    def from_side(k):
        return [same(k, back_side, core * half + side * quarter, quarter, side_peer)]

    def from_core(k):
        return [same(k, back_core, core * half, half, core_peer)]

    def begin(copies):
        for one in copies:
            one.start()

    def arrive(copies):
        for one in copies:
            one.wait_recv()

    def step_start(k):
        begin(to_core(k))

    def step_core(k):
        arrive(to_core(k))
        own = terms[:, span(k * rows + core * half, half), :]
        core_in[k] = (wide(own) + wide(core_in[k])).astype(core_in.dtype)
        begin(to_shard(k))

    def step_shard(k):
        arrive(to_shard(k))
        summed = wide(core_in[k, me])
        for i in range(shards - 1):
            summed = summed + wide(shard_in[k, i])
        core_in[k, me] = summed.astype(core_in.dtype)
        begin(to_side(k))

    def step_side(k):
        arrive(to_side(k))
        own = core_in[k, me, span(side * quarter, quarter), :]
        side_in[k] = (wide(own) + wide(side_in[k])).astype(side_in.dtype)
        begin(to_deep(k))

    def step_deep(k):
        arrive(to_deep(k))
        summed = wide(side_in[k, span(level * leaf, leaf), :])
        for i in range(depth - 1):
            summed = summed + wide(deep_in[k, i])
        start = k * rows + core * half + side * quarter + level * leaf
        total[span(start, leaf), :] = summed.astype(total.dtype)
        begin(from_deep(k))

    def step_back_deep(k):
        arrive(from_deep(k))
        begin(from_side(k))

    def step_back_side(k):
        arrive(from_side(k))
        begin(from_core(k))

    def step_back_core(k):
        arrive(from_core(k))
        for family in (to_core, to_shard, to_side, to_deep, from_deep, from_side, from_core):
            for one in family(k):
                one.wait_send()

    steps = (
        step_start,
        step_core,
        step_shard,
        step_side,
        step_deep,
        step_back_deep,
        step_back_side,
        step_back_core,
    )

    def tick(t, carry):
        for lag, step in enumerate(steps):
            k = t - lag

            @pl.when((k >= 0) & (k < chunks))
            def _(step=step, k=k):
                step(k)

        return carry

    lax.fori_loop(0, chunks + len(steps) - 1, tick, 0)


def sum_grads(matrices, gains, shards, replicas, identity):
    blocks = [
        matrix.astype(jnp.bfloat16).reshape(shards, matrix.shape[0] // shards, -1)
        for matrix in matrices
    ]
    if gains:
        line = jnp.concatenate([g.astype(jnp.bfloat16).reshape(shards, 1, -1) for g in gains], 2)
        blocks.append(jnp.pad(line, ((0, 0), (0, UNIT - 1), (0, PACK - line.shape[2]))))
    pieces = [block.shape[1] for block in blocks for _ in range(0, block.shape[2], PACK)]
    rows = UNIT * replicas
    chunks = -(-sum(pieces) // rows)
    depth = replicas // 4
    slots = shards + 2 * depth + 1
    kind = jnp.bfloat16
    count = len(blocks)
    total = pl.pallas_call(
        functools.partial(reduce_kernel, shards, depth, chunks, rows, count),
        out_shape=jax.ShapeDtypeStruct((chunks * rows, PACK), kind),
        in_specs=[pl.BlockSpec(memory_space=pl.ANY)] * count,
        out_specs=pl.BlockSpec(memory_space=pltpu.VMEM),
        scratch_shapes=[
            pltpu.VMEM((shards, chunks * rows, PACK), kind),
            pltpu.VMEM((chunks, shards, rows // 2, PACK), kind),
            pltpu.VMEM((chunks, shards - 1, rows // 2, PACK), kind),
            pltpu.VMEM((chunks, rows // 4, PACK), kind),
            pltpu.VMEM((chunks, depth - 1, UNIT, PACK), kind),
            pltpu.SemaphoreType.DMA((len(pieces),)),
            pltpu.SemaphoreType.DMA((chunks, slots)),
            pltpu.SemaphoreType.DMA((chunks, slots)),
        ],
        compiler_params=pltpu.CompilerParams(
            collective_id=identity, has_side_effects=True, vmem_limit_bytes=48 * 1024 * 1024
        ),
        name="reduce_terms",
    )(*blocks)
    results, start = [], 0
    for matrix in matrices:
        size = matrix.shape[0] // shards
        parts = []
        for _ in range(0, matrix.shape[1], PACK):
            parts.append(total[start : start + size].astype(jnp.float32))
            start += size
        results.append(jnp.concatenate(parts, 1))
    for i, gain in enumerate(gains):
        size = gain.shape[0] // shards
        results.append(total[start, i * size : (i + 1) * size].astype(jnp.float32))
    return results


def on_device(
    tokens,
    cotangent,
    positions,
    rest,
    first_gain,
    second_gain,
    merged_weight,
    output_weight,
    input_weight,
    down_weight,
):
    shards = lax.axis_size("shard")
    replicas = lax.axis_size("replica")
    gain_size = first_gain.shape[0]
    gains = jnp.concatenate([first_gain, second_gain])[None, :]
    gains = jnp.pad(gains, ((0, UNIT - 1), (0, -gains.shape[1] % 128)))
    fulls = gather_weights(
        [gains, merged_weight, output_weight, input_weight, down_weight], shards
    )
    gain_one = fulls[0][:, 0, :gain_size].reshape(-1)
    gain_two = fulls[0][:, 0, gain_size : 2 * gain_size].reshape(-1)
    merged_full, output_full, input_full, down_full = [
        full.reshape(-1, full.shape[2]) for full in fulls[1:]
    ]
    rows = tokens.shape[0]
    place = lax.axis_index(("replica", "shard"))
    count = lax.axis_size(("replica", "shard"))
    scale = HEAD_DIM ** (-0.5)
    tokens_f = tokens.astype(jnp.float32)
    norm_one, pull_one = jax.vjp(layer_norm, tokens_f, gain_one.astype(jnp.float32))
    norm_one_low = norm_one.astype(jnp.bfloat16)
    merged = jnp.dot(norm_one_low, merged_full, preferred_element_type=jnp.float32)
    cosine, sine = rotary_tables(positions)
    query = rotate(merged[:, :D].reshape(rows, HEADS, HEAD_DIM), cosine, sine).astype(jnp.bfloat16)
    keys = rotate(merged[:, D : 2 * D].reshape(rows, HEADS, HEAD_DIM), cosine, sine).astype(
        jnp.bfloat16
    )
    values = merged[:, 2 * D :].astype(jnp.bfloat16)
    pairs = jnp.concatenate([keys.reshape(rows, D), values], 1)
    pairs_wide = extended(pairs, ((("replica", "shard"), 0),), WINDOW)
    keys_wide = pairs_wide[:, :D].reshape(-1, HEADS, HEAD_DIM)
    values_wide = pairs_wide[:, D:].reshape(-1, HEADS, HEAD_DIM)
    allowed = window_mask(positions, rest, rows, place, count)[None]
    scores = (
        jnp.einsum("qhd,khd->hqk", query, keys_wide, preferred_element_type=jnp.float32) * scale
    )
    scores = jnp.where(allowed, scores, NEGATIVE)
    peak = jnp.max(scores, -1, keepdims=True)
    expo = jnp.exp(scores - peak)
    total = jnp.sum(expo, -1, keepdims=True)
    log_total = peak + jnp.log(total)
    prob = expo / total
    context = jnp.einsum(
        "hqk,khd->qhd", prob.astype(jnp.bfloat16), values_wide, preferred_element_type=jnp.float32
    )
    context = context.reshape(rows, D).astype(jnp.bfloat16)
    resid = tokens_f + jnp.dot(context, output_full, preferred_element_type=jnp.float32)
    norm_two, pull_two = jax.vjp(layer_norm, resid, gain_two.astype(jnp.float32))
    norm_two_low = norm_two.astype(jnp.bfloat16)
    hidden = jnp.dot(norm_two_low, input_full, preferred_element_type=jnp.float32)
    act, pull_act = jax.vjp(gated, hidden[:, :FF], hidden[:, FF:])
    act_low = act.astype(jnp.bfloat16)
    mixed = (resid + jnp.dot(act_low, down_full, preferred_element_type=jnp.float32)).astype(
        jnp.bfloat16
    )
    down_grad = jnp.einsum("tf,td->fd", act_low, cotangent, preferred_element_type=jnp.float32)
    grad_act = jnp.einsum("td,fd->tf", cotangent, down_full, preferred_element_type=jnp.float32)
    grad_gate, grad_up = pull_act(grad_act)
    grad_hidden = jnp.concatenate([grad_gate, grad_up], 1).astype(jnp.bfloat16)
    input_grad = jnp.einsum(
        "td,tf->df", norm_two_low, grad_hidden, preferred_element_type=jnp.float32
    )
    grad_norm_two = jnp.einsum(
        "tf,df->td", grad_hidden, input_full, preferred_element_type=jnp.float32
    )
    grad_resid_norm, second_gain_grad = pull_two(grad_norm_two)
    grad_resid = cotangent.astype(jnp.float32) + grad_resid_norm
    grad_resid_low = grad_resid.astype(jnp.bfloat16)
    output_grad = jnp.einsum(
        "td,te->de", context, grad_resid_low, preferred_element_type=jnp.float32
    )
    grad_context = jnp.einsum(
        "te,de->td", grad_resid_low, output_full, preferred_element_type=jnp.float32
    )
    grad_context = grad_context.astype(jnp.bfloat16).reshape(rows, HEADS, HEAD_DIM)
    scores_again = (
        jnp.einsum("qhd,khd->hqk", query, keys_wide, preferred_element_type=jnp.float32) * scale
    )
    scores_again = jnp.where(allowed, scores_again, NEGATIVE)
    prob_again = jnp.exp(scores_again - log_total)
    value_grad = jnp.einsum(
        "hqk,qhd->khd",
        prob_again.astype(jnp.bfloat16),
        grad_context,
        preferred_element_type=jnp.float32,
    )
    grad_prob = jnp.einsum(
        "qhd,khd->hqk", grad_context, values_wide, preferred_element_type=jnp.float32
    )
    grad_scores = prob_again * (grad_prob - jnp.sum(prob_again * grad_prob, -1, keepdims=True))
    grad_scores = grad_scores.astype(jnp.bfloat16)
    query_grad = (
        jnp.einsum("hqk,khd->qhd", grad_scores, keys_wide, preferred_element_type=jnp.float32)
        * scale
    )
    key_grad = (
        jnp.einsum("hqk,qhd->khd", grad_scores, query, preferred_element_type=jnp.float32) * scale
    )
    pair_grads = jnp.concatenate([key_grad.reshape(-1, D), value_grad.reshape(-1, D)], 1)
    middle = jnp.zeros((rows - 2 * WINDOW, 2 * D), jnp.float32)
    rims = jnp.concatenate([pair_grads[:WINDOW], middle, pair_grads[rows + WINDOW :]], 0)
    arrived = extended(rims.astype(jnp.bfloat16), ((("replica", "shard"), 0),), WINDOW).astype(
        rims.dtype
    )
    pair_own = pair_grads[WINDOW : rows + WINDOW] + jnp.concatenate(
        [arrived[:WINDOW], middle, arrived[rows + WINDOW :]], 0
    )
    grad_merged = jnp.concatenate(
        [
            unrotate(query_grad, cosine, sine).reshape(rows, D),
            unrotate(pair_own[:, :D].reshape(rows, HEADS, HEAD_DIM), cosine, sine).reshape(rows, D),
            pair_own[:, D:],
        ],
        1,
    ).astype(jnp.bfloat16)
    merged_grad = jnp.einsum(
        "td,te->de", norm_one_low, grad_merged, preferred_element_type=jnp.float32
    )
    grad_norm_one = jnp.einsum(
        "te,de->td", grad_merged, merged_full, preferred_element_type=jnp.float32
    )
    grad_tokens_norm, first_gain_grad = pull_one(grad_norm_one)
    token_grad = grad_resid + grad_tokens_norm
    merged_sum, output_sum, input_sum, down_sum, first_sum, second_sum = sum_grads(
        [merged_grad, output_grad, input_grad, down_grad],
        [first_gain_grad, second_gain_grad],
        shards,
        replicas,
        1,
    )
    return (
        mixed,
        token_grad,
        first_sum,
        second_sum,
        merged_sum,
        output_sum,
        input_sum,
        down_sum,
    )


def solution(mesh):
    return jax.shard_map(
        on_device,
        mesh=mesh,
        in_specs=(
            P(("replica", "shard"), None),
            P(("replica", "shard"), None),
            P(("replica", "shard")),
            P(("replica", "shard")),
            P("shard"),
            P("shard"),
            P("shard", None),
            P("shard", None),
            P("shard", None),
            P("shard", None),
        ),
        out_specs=(
            P(("replica", "shard"), None),
            P(("replica", "shard"), None),
            P("shard"),
            P("shard"),
            P("shard", None),
            P("shard", None),
            P("shard", None),
            P("shard", None),
        ),
        check_vma=False,
    )
```

```python
import functools
import math

import jax
import jax.numpy as jnp
from jax import lax
from jax.experimental import pallas as pl
from jax.experimental.pallas import tpu as pltpu
from jax.sharding import PartitionSpec as P

D = 768
HEADS = 12
HEAD_DIM = 64
FF = 1152
WINDOW = 64


EPSILON = 1e-05
NEGATIVE = -1e30


def extended(cells, sides, width):
    for axis, dim in sides:
        count = lax.axis_size(axis)
        ends = count - 1
        head = lax.slice_in_dim(cells, 0, width, axis=dim)
        tail = lax.slice_in_dim(cells, cells.shape[dim] - width, cells.shape[dim], axis=dim)
        cells = jnp.concatenate(
            [
                lax.ppermute(tail, axis, [(i, (i + 1) % count) for i in range(ends)]),
                cells,
                lax.ppermute(head, axis, [((i + 1) % count, i) for i in range(ends)]),
            ],
            axis=dim,
        )
    return cells


def layer_norm(values, gain):
    centre = values - jnp.mean(values, -1, keepdims=True)
    spread = jnp.mean(centre * centre, -1, keepdims=True)
    return centre * lax.rsqrt(spread + EPSILON) * gain


def rotary_tables(positions):
    half = HEAD_DIM // 2
    freqs = jnp.exp(jnp.arange(half, dtype=jnp.float32) * (-2.0 * math.log(10000.0) / HEAD_DIM))
    angles = positions.astype(jnp.float32)[:, None] * freqs[None, :]
    angles = jnp.concatenate([angles, angles], -1)[:, None, :]
    return (jnp.cos(angles), jnp.sin(angles))


def rotate(values, cosine, sine):
    half = values.shape[-1] // 2
    turned = jnp.concatenate([-values[..., half:], values[..., :half]], -1)
    return values * cosine + turned * sine


def unrotate(grads, cosine, sine):
    pull = jax.vjp(lambda inner: rotate(inner, cosine, sine), grads)[1]
    return pull(grads)[0]


def gated(gate, up):
    return jax.nn.gelu(gate, approximate=False) * up


def window_mask(positions, rest, rows, place, count):
    query_rows = jnp.arange(rows, dtype=jnp.int32)[:, None]
    key_cols = jnp.arange(rows + 2 * WINDOW, dtype=jnp.int32)[None, :]
    offset = key_cols - WINDOW - query_rows
    allowed = (
        (jnp.abs(offset) <= WINDOW) & (-offset <= positions[:, None]) & (offset <= rest[:, None])
    )
    allowed = allowed & ((key_cols >= WINDOW) | (place > 0))
    allowed = allowed & ((key_cols < rows + WINDOW) | (place < count - 1))
    return allowed


PACK = 384
UNIT = 16
MESH = pl.DeviceIdType.MESH


def greet(peers):
    barrier = pltpu.get_barrier_semaphore()
    for peer in peers:
        pl.semaphore_signal(barrier, inc=1, device_id=peer, device_id_type=MESH)
    pl.semaphore_wait(barrier, len(peers))


def gather_kernel(shards, splits, *refs):
    count = len(splits)
    sources, fulls = refs[:count], refs[count : 2 * count]
    send_sem, recv_sem = refs[2 * count :]
    replica = lax.axis_index("replica")
    me = lax.axis_index("shard")
    core = lax.rem(replica, 2)
    side = lax.rem(lax.div(replica, 2), 2)
    core_peer = (replica + 1 - 2 * core, me)
    side_peer = (replica + 2 - 4 * side, me)
    greet(
        [(replica, lax.rem(me + off, shards)) for off in range(1, shards)] + [core_peer, side_peer]
    )

    def part(which, row_half, col_half):
        rows, cols = sources[which].shape
        by_rows, by_cols = splits[which]
        take_rows, take_cols = pl.ds(0, rows), pl.ds(0, cols)
        if by_rows:
            take_rows = pl.ds(pl.multiple_of(row_half * (rows // 2), UNIT), rows // 2)
        if by_cols:
            take_cols = pl.ds(pl.multiple_of(col_half * (cols // 2), 128), cols // 2)
        return take_rows, take_cols

    def copy(which, off, kind, source, target, peer):
        return pltpu.make_async_remote_copy(
            src_ref=source,
            dst_ref=target,
            send_sem=send_sem.at[which, off - 1, kind],
            recv_sem=recv_sem.at[which, off - 1, kind],
            device_id=peer,
            device_id_type=MESH,
        )

    def place(which, owner, row_half, col_half):
        return fulls[which].at[(owner,) + part(which, row_half, col_half)]

    copies = {}
    for which in range(count):
        for off in range(1, shards):
            copies[which, off, 0] = copy(
                which,
                off,
                0,
                sources[which].at[part(which, side, core)],
                place(which, me, side, core),
                (replica, lax.rem(me + off, shards)),
            )
            copies[which, off, 0].start()
    for which in range(count):
        fulls[which][me] = sources[which][...]

    def forward(which):
        by_rows, by_cols = splits[which]
        for off in range(1, shards):
            owner = lax.rem(me + shards - off, shards)
            piece = place(which, owner, side, core)
            copies[which, off, 0].wait_recv()
            if by_rows:
                copies[which, off, 1] = copy(which, off, 1, piece, piece, side_peer)
                copies[which, off, 1].start()
            if by_cols:
                copies[which, off, 2] = copy(which, off, 2, piece, piece, core_peer)
                copies[which, off, 2].start()

    def cross(which):
        by_rows, by_cols = splits[which]
        for off in range(1, shards):
            owner = lax.rem(me + shards - off, shards)
            if by_rows:
                copies[which, off, 1].wait_recv()
                if by_cols:
                    piece = place(which, owner, 1 - side, core)
                    copies[which, off, 3] = copy(which, off, 3, piece, piece, core_peer)
                    copies[which, off, 3].start()

    for which in range(count + 1):
        if which < count:
            forward(which)
        if which > 0:
            cross(which - 1)
    for which in range(count):
        for off in range(1, shards):
            for kind in (2, 3):
                if (which, off, kind) in copies:
                    copies[which, off, kind].wait_recv()
    for one in copies.values():
        one.wait_send()


def gather_weights(weights, shards):
    splits = tuple(
        (w.shape[0] % (2 * UNIT) == 0, w.shape[1] % 256 == 0 and w.shape[0] > UNIT)
        for w in weights
    )
    count = len(weights)
    fulls = pl.pallas_call(
        functools.partial(gather_kernel, shards, splits),
        out_shape=[jax.ShapeDtypeStruct((shards,) + w.shape, w.dtype) for w in weights],
        in_specs=[pl.BlockSpec(memory_space=pltpu.VMEM)] * count,
        out_specs=[pl.BlockSpec(memory_space=pltpu.VMEM)] * count,
        scratch_shapes=[
            pltpu.SemaphoreType.DMA((count, shards - 1, 4)),
            pltpu.SemaphoreType.DMA((count, shards - 1, 4)),
        ],
        compiler_params=pltpu.CompilerParams(
            collective_id=0, has_side_effects=True, vmem_limit_bytes=40 * 1024 * 1024
        ),
        name="gather_weights",
    )(*weights)
    return fulls


def reduce_kernel(shards, depth, chunks, rows, count, *refs):
    matrices, total = refs[:count], refs[count]
    terms, core_in, shard_in, side_in, deep_in, packs, sends, recvs = refs[count + 1 :]
    loads, filled = [], 0
    for matrix in matrices:
        taken = matrix.shape[1]
        for left in range(0, matrix.shape[2], PACK):
            load = pltpu.make_async_copy(
                matrix.at[:, :, pl.ds(left, PACK)],
                terms.at[:, pl.ds(filled, taken), :],
                packs.at[len(loads)],
            )
            load.start()
            filled += taken
            loads.append((load, filled))
    if filled < chunks * rows:
        terms[:, filled:, :] = jnp.zeros((shards, chunks * rows - filled, PACK), terms.dtype)
    replica = lax.axis_index("replica")
    me = lax.axis_index("shard")
    core = lax.rem(replica, 2)
    side = lax.rem(lax.div(replica, 2), 2)
    level = lax.div(replica, 4)
    half, quarter, leaf = rows // 2, rows // 4, rows // (4 * depth)
    core_peer = (replica + 1 - 2 * core, me)
    side_peer = (replica + 2 - 4 * side, me)
    shard_peers = [(replica, lax.rem(me + off, shards)) for off in range(1, shards)]
    levels = [lax.rem(level + off, depth) for off in range(1, depth)]
    deep_peers = [(4 * other + lax.rem(replica, 4), me) for other in levels]
    greet([core_peer, side_peer] + shard_peers + deep_peers)
    first_shard, first_side, first_deep = 1, shards, shards + 1
    back_deep, back_side, back_core = shards + depth, shards + 2 * depth - 1, shards + 2 * depth

    def copy(chunk, slot, source, target, peer):
        return pltpu.make_async_remote_copy(
            src_ref=source,
            dst_ref=target,
            send_sem=sends.at[chunk, slot],
            recv_sem=recvs.at[chunk, slot],
            device_id=peer,
            device_id_type=MESH,
        )

    def span(start, size):
        return pl.ds(pl.multiple_of(start, UNIT), size)

    def wide(cells):
        return cells.astype(jnp.float32)

    def to_core(k):
        source = terms.at[:, span(k * rows + (1 - core) * half, half), :]
        return [copy(k, 0, source, core_in.at[k], core_peer)]

    def to_shard(k):
        return [
            copy(
                k,
                first_shard + i,
                core_in.at[k, lax.rem(me + i + 1, shards)],
                shard_in.at[k, i],
                shard_peers[i],
            )
            for i in range(shards - 1)
        ]

    def to_side(k):
        source = core_in.at[k, me, span((1 - side) * quarter, quarter), :]
        return [copy(k, first_side, source, side_in.at[k], side_peer)]

    def to_deep(k):
        return [
            copy(
                k,
                first_deep + i,
                side_in.at[k, span(levels[i] * leaf, leaf), :],
                deep_in.at[k, i],
                deep_peers[i],
            )
            for i in range(depth - 1)
        ]

    def same(k, slot, start, size, peer):
        region = total.at[span(k * rows + start, size), :]
        return copy(k, slot, region, region, peer)

    def from_deep(k):
        start = core * half + side * quarter + level * leaf
        return [same(k, back_deep + i, start, leaf, deep_peers[i]) for i in range(depth - 1)]

    def from_side(k):
        return [same(k, back_side, core * half + side * quarter, quarter, side_peer)]

    def from_core(k):
        return [same(k, back_core, core * half, half, core_peer)]

    def begin(copies):
        for one in copies:
            one.start()

    def arrive(copies):
        for one in copies:
            one.wait_recv()

    def step_core(k):
        arrive(to_core(k))
        own = terms[:, span(k * rows + core * half, half), :]
        core_in[k] = (wide(own) + wide(core_in[k])).astype(core_in.dtype)
        begin(to_shard(k))

    def step_shard(k):
        arrive(to_shard(k))
        summed = wide(core_in[k, me])
        for i in range(shards - 1):
            summed = summed + wide(shard_in[k, i])
        core_in[k, me] = summed.astype(core_in.dtype)
        begin(to_side(k))

    def step_side(k):
        arrive(to_side(k))
        own = core_in[k, me, span(side * quarter, quarter), :]
        side_in[k] = (wide(own) + wide(side_in[k])).astype(side_in.dtype)
        begin(to_deep(k))

    def step_deep(k):
        arrive(to_deep(k))
        summed = wide(side_in[k, span(level * leaf, leaf), :])
        for i in range(depth - 1):
            summed = summed + wide(deep_in[k, i])
        start = k * rows + core * half + side * quarter + level * leaf
        total[span(start, leaf), :] = summed.astype(total.dtype)
        begin(from_deep(k))

    def step_back_deep(k):
        arrive(from_deep(k))
        begin(from_side(k))

    def step_back_side(k):
        arrive(from_side(k))
        begin(from_core(k))

    def step_back_core(k):
        arrive(from_core(k))
        for family in (to_core, to_shard, to_side, to_deep, from_deep, from_side, from_core):
            for one in family(k):
                one.wait_send()

    steps = (
        step_core,
        step_shard,
        step_side,
        step_deep,
        step_back_deep,
        step_back_side,
        step_back_core,
    )

    def tick(t, carry):
        for lag, step in enumerate(steps):
            k = t - lag

            @pl.when((k >= 0) & (k < chunks))
            def _(step=step, k=k):
                step(k)

        return carry

    sent = 0
    for load, ready in loads:
        load.wait()
        while (sent + 1) * rows <= ready:
            begin(to_core(sent))
            sent += 1
    for k in range(sent, chunks):
        begin(to_core(k))
    lax.fori_loop(0, chunks + len(steps) - 1, tick, 0)


def sum_grads(matrices, gains, shards, replicas, identity):
    blocks = [
        matrix.astype(jnp.bfloat16).reshape(shards, matrix.shape[0] // shards, -1)
        for matrix in matrices
    ]
    if gains:
        lines = jnp.concatenate([g.astype(jnp.bfloat16).reshape(shards, 1, -1) for g in gains], 1)
        short = (UNIT - len(gains), PACK - lines.shape[2])
        blocks.append(jnp.pad(lines, ((0, 0), (0, short[0]), (0, short[1]))))
    pieces = [block.shape[1] for block in blocks for _ in range(0, block.shape[2], PACK)]
    rows = UNIT * replicas
    chunks = -(-sum(pieces) // rows)
    depth = replicas // 4
    slots = shards + 2 * depth + 1
    kind = jnp.bfloat16
    count = len(blocks)
    total = pl.pallas_call(
        functools.partial(reduce_kernel, shards, depth, chunks, rows, count),
        out_shape=jax.ShapeDtypeStruct((chunks * rows, PACK), kind),
        in_specs=[pl.BlockSpec(memory_space=pl.ANY)] * count,
        out_specs=pl.BlockSpec(memory_space=pltpu.VMEM),
        scratch_shapes=[
            pltpu.VMEM((shards, chunks * rows, PACK), kind),
            pltpu.VMEM((chunks, shards, rows // 2, PACK), kind),
            pltpu.VMEM((chunks, shards - 1, rows // 2, PACK), kind),
            pltpu.VMEM((chunks, rows // 4, PACK), kind),
            pltpu.VMEM((chunks, depth - 1, UNIT, PACK), kind),
            pltpu.SemaphoreType.DMA((len(pieces),)),
            pltpu.SemaphoreType.DMA((chunks, slots)),
            pltpu.SemaphoreType.DMA((chunks, slots)),
        ],
        compiler_params=pltpu.CompilerParams(
            collective_id=identity, has_side_effects=True, vmem_limit_bytes=48 * 1024 * 1024
        ),
        name="reduce_terms",
    )(*blocks)
    results, start = [], 0
    for matrix in matrices:
        size = matrix.shape[0] // shards
        parts = []
        for _ in range(0, matrix.shape[1], PACK):
            parts.append(total[start : start + size].astype(jnp.float32))
            start += size
        results.append(jnp.concatenate(parts, 1))
    for i, gain in enumerate(gains):
        size = gain.shape[0] // shards
        results.append(total[start + i, :size].astype(jnp.float32))
    return results


def on_device(
    tokens,
    cotangent,
    positions,
    rest,
    first_gain,
    second_gain,
    merged_weight,
    output_weight,
    input_weight,
    down_weight,
):
    shards = lax.axis_size("shard")
    replicas = lax.axis_size("replica")
    gain_size = first_gain.shape[0]
    gains = jnp.concatenate([first_gain, second_gain])[None, :]
    gains = jnp.pad(gains, ((0, UNIT - 1), (0, -gains.shape[1] % 128)))
    fulls = gather_weights(
        [gains, merged_weight, output_weight, input_weight, down_weight], shards
    )
    gain_one = fulls[0][:, 0, :gain_size].reshape(-1)
    gain_two = fulls[0][:, 0, gain_size : 2 * gain_size].reshape(-1)
    merged_full, output_full, input_full, down_full = [
        full.reshape(-1, full.shape[2]) for full in fulls[1:]
    ]
    rows = tokens.shape[0]
    place = lax.axis_index(("replica", "shard"))
    count = lax.axis_size(("replica", "shard"))
    scale = HEAD_DIM ** (-0.5)
    tokens_f = tokens.astype(jnp.float32)
    norm_one, pull_one = jax.vjp(layer_norm, tokens_f, gain_one.astype(jnp.float32))
    norm_one_low = norm_one.astype(jnp.bfloat16)
    merged = jnp.dot(norm_one_low, merged_full, preferred_element_type=jnp.float32)
    cosine, sine = rotary_tables(positions)
    query = rotate(merged[:, :D].reshape(rows, HEADS, HEAD_DIM), cosine, sine).astype(jnp.bfloat16)
    keys = rotate(merged[:, D : 2 * D].reshape(rows, HEADS, HEAD_DIM), cosine, sine).astype(
        jnp.bfloat16
    )
    values = merged[:, 2 * D :].astype(jnp.bfloat16)
    pairs = jnp.concatenate([keys.reshape(rows, D), values], 1)
    pairs_wide = extended(pairs, ((("replica", "shard"), 0),), WINDOW)
    keys_wide = pairs_wide[:, :D].reshape(-1, HEADS, HEAD_DIM)
    values_wide = pairs_wide[:, D:].reshape(-1, HEADS, HEAD_DIM)
    allowed = window_mask(positions, rest, rows, place, count)[None]
    scores = (
        jnp.einsum("qhd,khd->hqk", query, keys_wide, preferred_element_type=jnp.float32) * scale
    )
    scores = jnp.where(allowed, scores, NEGATIVE)
    peak = jnp.max(scores, -1, keepdims=True)
    expo = jnp.exp(scores - peak)
    total = jnp.sum(expo, -1, keepdims=True)
    log_total = peak + jnp.log(total)
    prob = expo / total
    context = jnp.einsum(
        "hqk,khd->qhd", prob.astype(jnp.bfloat16), values_wide, preferred_element_type=jnp.float32
    )
    context = context.reshape(rows, D).astype(jnp.bfloat16)
    resid = tokens_f + jnp.dot(context, output_full, preferred_element_type=jnp.float32)
    norm_two, pull_two = jax.vjp(layer_norm, resid, gain_two.astype(jnp.float32))
    norm_two_low = norm_two.astype(jnp.bfloat16)
    hidden = jnp.dot(norm_two_low, input_full, preferred_element_type=jnp.float32)
    act, pull_act = jax.vjp(gated, hidden[:, :FF], hidden[:, FF:])
    act_low = act.astype(jnp.bfloat16)
    mixed = (resid + jnp.dot(act_low, down_full, preferred_element_type=jnp.float32)).astype(
        jnp.bfloat16
    )
    down_grad = jnp.einsum("tf,td->fd", act_low, cotangent, preferred_element_type=jnp.float32)
    grad_act = jnp.einsum("td,fd->tf", cotangent, down_full, preferred_element_type=jnp.float32)
    grad_gate, grad_up = pull_act(grad_act)
    grad_hidden = jnp.concatenate([grad_gate, grad_up], 1).astype(jnp.bfloat16)
    input_grad = jnp.einsum(
        "td,tf->df", norm_two_low, grad_hidden, preferred_element_type=jnp.float32
    )
    grad_norm_two = jnp.einsum(
        "tf,df->td", grad_hidden, input_full, preferred_element_type=jnp.float32
    )
    grad_resid_norm, second_gain_grad = pull_two(grad_norm_two)
    grad_resid = cotangent.astype(jnp.float32) + grad_resid_norm
    grad_resid_low = grad_resid.astype(jnp.bfloat16)
    output_grad = jnp.einsum(
        "td,te->de", context, grad_resid_low, preferred_element_type=jnp.float32
    )
    grad_context = jnp.einsum(
        "te,de->td", grad_resid_low, output_full, preferred_element_type=jnp.float32
    )
    grad_context = grad_context.astype(jnp.bfloat16).reshape(rows, HEADS, HEAD_DIM)
    scores_again = (
        jnp.einsum("qhd,khd->hqk", query, keys_wide, preferred_element_type=jnp.float32) * scale
    )
    scores_again = jnp.where(allowed, scores_again, NEGATIVE)
    prob_again = jnp.exp(scores_again - log_total)
    value_grad = jnp.einsum(
        "hqk,qhd->khd",
        prob_again.astype(jnp.bfloat16),
        grad_context,
        preferred_element_type=jnp.float32,
    )
    grad_prob = jnp.einsum(
        "qhd,khd->hqk", grad_context, values_wide, preferred_element_type=jnp.float32
    )
    grad_scores = prob_again * (grad_prob - jnp.sum(prob_again * grad_prob, -1, keepdims=True))
    grad_scores = grad_scores.astype(jnp.bfloat16)
    query_grad = (
        jnp.einsum("hqk,khd->qhd", grad_scores, keys_wide, preferred_element_type=jnp.float32)
        * scale
    )
    key_grad = (
        jnp.einsum("hqk,qhd->khd", grad_scores, query, preferred_element_type=jnp.float32) * scale
    )
    pair_grads = jnp.concatenate([key_grad.reshape(-1, D), value_grad.reshape(-1, D)], 1)
    middle = jnp.zeros((rows - 2 * WINDOW, 2 * D), jnp.float32)
    rims = jnp.concatenate([pair_grads[:WINDOW], middle, pair_grads[rows + WINDOW :]], 0)
    arrived = extended(rims.astype(jnp.bfloat16), ((("replica", "shard"), 0),), WINDOW).astype(
        rims.dtype
    )
    pair_own = pair_grads[WINDOW : rows + WINDOW] + jnp.concatenate(
        [arrived[:WINDOW], middle, arrived[rows + WINDOW :]], 0
    )
    grad_merged = jnp.concatenate(
        [
            unrotate(query_grad, cosine, sine).reshape(rows, D),
            unrotate(pair_own[:, :D].reshape(rows, HEADS, HEAD_DIM), cosine, sine).reshape(rows, D),
            pair_own[:, D:],
        ],
        1,
    ).astype(jnp.bfloat16)
    merged_grad = jnp.einsum(
        "td,te->de", norm_one_low, grad_merged, preferred_element_type=jnp.float32
    )
    grad_norm_one = jnp.einsum(
        "te,de->td", grad_merged, merged_full, preferred_element_type=jnp.float32
    )
    grad_tokens_norm, first_gain_grad = pull_one(grad_norm_one)
    token_grad = grad_resid + grad_tokens_norm
    merged_sum, output_sum, input_sum, down_sum, first_sum, second_sum = sum_grads(
        [merged_grad, output_grad, input_grad, down_grad],
        [first_gain_grad, second_gain_grad],
        shards,
        replicas,
        1,
    )
    return (
        mixed,
        token_grad,
        first_sum,
        second_sum,
        merged_sum,
        output_sum,
        input_sum,
        down_sum,
    )


def solution(mesh):
    return jax.shard_map(
        on_device,
        mesh=mesh,
        in_specs=(
            P(("replica", "shard"), None),
            P(("replica", "shard"), None),
            P(("replica", "shard")),
            P(("replica", "shard")),
            P("shard"),
            P("shard"),
            P("shard", None),
            P("shard", None),
            P("shard", None),
            P("shard", None),
        ),
        out_specs=(
            P(("replica", "shard"), None),
            P(("replica", "shard"), None),
            P("shard"),
            P("shard"),
            P("shard", None),
            P("shard", None),
            P("shard", None),
            P("shard", None),
        ),
        check_vma=False,
    )
```

```python
import functools
import math

import jax
import jax.numpy as jnp
from jax import lax
from jax.experimental import pallas as pl
from jax.experimental.pallas import tpu as pltpu
from jax.sharding import PartitionSpec as P

D = 768
HEADS = 12
HEAD_DIM = 64
FF = 1152
WINDOW = 64


EPSILON = 1e-05
NEGATIVE = -1e30


def extended(cells, sides, width):
    for axis, dim in sides:
        count = lax.axis_size(axis)
        ends = count - 1
        head = lax.slice_in_dim(cells, 0, width, axis=dim)
        tail = lax.slice_in_dim(cells, cells.shape[dim] - width, cells.shape[dim], axis=dim)
        cells = jnp.concatenate(
            [
                lax.ppermute(tail, axis, [(i, (i + 1) % count) for i in range(ends)]),
                cells,
                lax.ppermute(head, axis, [((i + 1) % count, i) for i in range(ends)]),
            ],
            axis=dim,
        )
    return cells


def layer_norm(values, gain):
    centre = values - jnp.mean(values, -1, keepdims=True)
    spread = jnp.mean(centre * centre, -1, keepdims=True)
    return centre * lax.rsqrt(spread + EPSILON) * gain


def rotary_tables(positions):
    half = HEAD_DIM // 2
    freqs = jnp.exp(jnp.arange(half, dtype=jnp.float32) * (-2.0 * math.log(10000.0) / HEAD_DIM))
    angles = positions.astype(jnp.float32)[:, None] * freqs[None, :]
    angles = jnp.concatenate([angles, angles], -1)[:, None, :]
    return (jnp.cos(angles), jnp.sin(angles))


def rotate(values, cosine, sine):
    half = values.shape[-1] // 2
    turned = jnp.concatenate([-values[..., half:], values[..., :half]], -1)
    return values * cosine + turned * sine


def unrotate(grads, cosine, sine):
    pull = jax.vjp(lambda inner: rotate(inner, cosine, sine), grads)[1]
    return pull(grads)[0]


def gated(gate, up):
    return jax.nn.gelu(gate, approximate=False) * up


def window_mask(positions, rest, rows, place, count):
    query_rows = jnp.arange(rows, dtype=jnp.int32)[:, None]
    key_cols = jnp.arange(rows + 2 * WINDOW, dtype=jnp.int32)[None, :]
    offset = key_cols - WINDOW - query_rows
    allowed = (
        (jnp.abs(offset) <= WINDOW) & (-offset <= positions[:, None]) & (offset <= rest[:, None])
    )
    allowed = allowed & ((key_cols >= WINDOW) | (place > 0))
    allowed = allowed & ((key_cols < rows + WINDOW) | (place < count - 1))
    return allowed


PACK = 768
UNIT = 16
MESH = pl.DeviceIdType.MESH


def greet(peers):
    barrier = pltpu.get_barrier_semaphore()
    for peer in peers:
        pl.semaphore_signal(barrier, inc=1, device_id=peer, device_id_type=MESH)
    pl.semaphore_wait(barrier, len(peers))


def gather_kernel(shards, splits, *refs):
    count = len(splits)
    sources, fulls = refs[:count], refs[count : 2 * count]
    keep_sem, send_sem, recv_sem = refs[2 * count :]
    replica = lax.axis_index("replica")
    me = lax.axis_index("shard")
    core = lax.rem(replica, 2)
    side = lax.rem(lax.div(replica, 2), 2)
    core_peer = (replica + 1 - 2 * core, me)
    side_peer = (replica + 2 - 4 * side, me)
    greet(
        [(replica, lax.rem(me + off, shards)) for off in range(1, shards)] + [core_peer, side_peer]
    )

    def part(which, row_half, col_half):
        rows, cols = sources[which].shape
        by_rows, by_cols = splits[which]
        take_rows, take_cols = pl.ds(0, rows), pl.ds(0, cols)
        if by_rows:
            take_rows = pl.ds(pl.multiple_of(row_half * (rows // 2), UNIT), rows // 2)
        if by_cols:
            take_cols = pl.ds(pl.multiple_of(col_half * (cols // 2), 128), cols // 2)
        return take_rows, take_cols

    def copy(which, off, kind, source, target, peer):
        return pltpu.make_async_remote_copy(
            src_ref=source,
            dst_ref=target,
            send_sem=send_sem.at[which, off - 1, kind],
            recv_sem=recv_sem.at[which, off - 1, kind],
            device_id=peer,
            device_id_type=MESH,
        )

    def place(which, owner, row_half, col_half):
        return fulls[which].at[(owner,) + part(which, row_half, col_half)]

    copies = {}
    for which in range(count):
        for off in range(1, shards):
            copies[which, off, 0] = copy(
                which,
                off,
                0,
                sources[which].at[part(which, side, core)],
                place(which, me, side, core),
                (replica, lax.rem(me + off, shards)),
            )
            copies[which, off, 0].start()
    keeps = []
    for which in range(count):
        keep = pltpu.make_async_copy(sources[which], fulls[which].at[me], keep_sem.at[which])
        keep.start()
        keeps.append(keep)

    def forward(which):
        by_rows, by_cols = splits[which]
        for off in range(1, shards):
            owner = lax.rem(me + shards - off, shards)
            piece = place(which, owner, side, core)
            copies[which, off, 0].wait_recv()
            if by_rows:
                copies[which, off, 1] = copy(which, off, 1, piece, piece, side_peer)
                copies[which, off, 1].start()
            if by_cols:
                copies[which, off, 2] = copy(which, off, 2, piece, piece, core_peer)
                copies[which, off, 2].start()

    def cross(which):
        by_rows, by_cols = splits[which]
        for off in range(1, shards):
            owner = lax.rem(me + shards - off, shards)
            if by_rows:
                copies[which, off, 1].wait_recv()
                if by_cols:
                    piece = place(which, owner, 1 - side, core)
                    copies[which, off, 3] = copy(which, off, 3, piece, piece, core_peer)
                    copies[which, off, 3].start()

    for which in range(count + 1):
        if which < count:
            forward(which)
        if which > 0:
            cross(which - 1)
    for which in range(count):
        for off in range(1, shards):
            for kind in (2, 3):
                if (which, off, kind) in copies:
                    copies[which, off, kind].wait_recv()
    for keep in keeps:
        keep.wait()
    for one in copies.values():
        one.wait_send()


def gather_weights(weights, shards):
    splits = tuple(
        (w.shape[0] % (2 * UNIT) == 0, w.shape[1] % 256 == 0 and w.shape[0] > UNIT)
        for w in weights
    )
    count = len(weights)
    fulls = pl.pallas_call(
        functools.partial(gather_kernel, shards, splits),
        out_shape=[jax.ShapeDtypeStruct((shards,) + w.shape, w.dtype) for w in weights],
        in_specs=[pl.BlockSpec(memory_space=pltpu.HBM)] * count,
        out_specs=[pl.BlockSpec(memory_space=pltpu.VMEM)] * count,
        scratch_shapes=[
            pltpu.SemaphoreType.DMA((count,)),
            pltpu.SemaphoreType.DMA((count, shards - 1, 4)),
            pltpu.SemaphoreType.DMA((count, shards - 1, 4)),
        ],
        compiler_params=pltpu.CompilerParams(
            collective_id=0, has_side_effects=True, vmem_limit_bytes=40 * 1024 * 1024
        ),
        name="gather_weights",
    )(*weights)
    return fulls


def reduce_kernel(shards, depth, chunks, rows, count, *refs):
    matrices, total = refs[:count], refs[count]
    terms, core_in, shard_in, side_in, deep_in, packs, sends, recvs = refs[count + 1 :]
    loads, filled = [], 0
    for matrix in matrices:
        taken = matrix.shape[1]
        for left in range(0, matrix.shape[2], PACK):
            load = pltpu.make_async_copy(
                matrix.at[:, :, pl.ds(left, PACK)],
                terms.at[:, pl.ds(filled, taken), :],
                packs.at[len(loads)],
            )
            load.start()
            loads.append(load)
            filled += taken
    if filled < chunks * rows:
        terms[:, filled:, :] = jnp.zeros((shards, chunks * rows - filled, PACK), terms.dtype)
    replica = lax.axis_index("replica")
    me = lax.axis_index("shard")
    core = lax.rem(replica, 2)
    side = lax.rem(lax.div(replica, 2), 2)
    level = lax.div(replica, 4)
    half, quarter, leaf = rows // 2, rows // 4, rows // (4 * depth)
    core_peer = (replica + 1 - 2 * core, me)
    side_peer = (replica + 2 - 4 * side, me)
    shard_peers = [(replica, lax.rem(me + off, shards)) for off in range(1, shards)]
    levels = [lax.rem(level + off, depth) for off in range(1, depth)]
    deep_peers = [(4 * other + lax.rem(replica, 4), me) for other in levels]
    greet([core_peer, side_peer] + shard_peers + deep_peers)
    for load in loads:
        load.wait()
    first_shard, first_side, first_deep = 1, shards, shards + 1
    back_deep, back_side, back_core = shards + depth, shards + 2 * depth - 1, shards + 2 * depth

    def copy(chunk, slot, source, target, peer):
        return pltpu.make_async_remote_copy(
            src_ref=source,
            dst_ref=target,
            send_sem=sends.at[chunk, slot],
            recv_sem=recvs.at[chunk, slot],
            device_id=peer,
            device_id_type=MESH,
        )

    def span(start, size):
        return pl.ds(pl.multiple_of(start, UNIT), size)

    def wide(cells):
        return cells.astype(jnp.float32)

    def to_core(k):
        source = terms.at[:, span(k * rows + (1 - core) * half, half), :]
        return [copy(k, 0, source, core_in.at[k], core_peer)]

    def to_shard(k):
        return [
            copy(
                k,
                first_shard + i,
                core_in.at[k, lax.rem(me + i + 1, shards)],
                shard_in.at[k, i],
                shard_peers[i],
            )
            for i in range(shards - 1)
        ]

    def to_side(k):
        source = core_in.at[k, me, span((1 - side) * quarter, quarter), :]
        return [copy(k, first_side, source, side_in.at[k], side_peer)]

    def to_deep(k):
        return [
            copy(
                k,
                first_deep + i,
                side_in.at[k, span(levels[i] * leaf, leaf), :],
                deep_in.at[k, i],
                deep_peers[i],
            )
            for i in range(depth - 1)
        ]

    def same(k, slot, start, size, peer):
        region = total.at[span(k * rows + start, size), :]
        return copy(k, slot, region, region, peer)

    def from_deep(k):
        start = core * half + side * quarter + level * leaf
        return [same(k, back_deep + i, start, leaf, deep_peers[i]) for i in range(depth - 1)]

    def from_side(k):
        return [same(k, back_side, core * half + side * quarter, quarter, side_peer)]

    def from_core(k):
        return [same(k, back_core, core * half, half, core_peer)]

    def begin(copies):
        for one in copies:
            one.start()

    def arrive(copies):
        for one in copies:
            one.wait_recv()

    def step_start(k):
        begin(to_core(k))

    def step_core(k):
        arrive(to_core(k))
        own = terms[:, span(k * rows + core * half, half), :]
        core_in[k] = (wide(own) + wide(core_in[k])).astype(core_in.dtype)
        begin(to_shard(k))

    def step_shard(k):
        arrive(to_shard(k))
        summed = wide(core_in[k, me])
        for i in range(shards - 1):
            summed = summed + wide(shard_in[k, i])
        core_in[k, me] = summed.astype(core_in.dtype)
        begin(to_side(k))

    def step_side(k):
        arrive(to_side(k))
        own = core_in[k, me, span(side * quarter, quarter), :]
        side_in[k] = (wide(own) + wide(side_in[k])).astype(side_in.dtype)
        begin(to_deep(k))

    def step_deep(k):
        arrive(to_deep(k))
        summed = wide(side_in[k, span(level * leaf, leaf), :])
        for i in range(depth - 1):
            summed = summed + wide(deep_in[k, i])
        start = k * rows + core * half + side * quarter + level * leaf
        total[span(start, leaf), :] = summed.astype(total.dtype)
        begin(from_deep(k))

    def step_back_deep(k):
        arrive(from_deep(k))
        begin(from_side(k))

    def step_back_side(k):
        arrive(from_side(k))
        begin(from_core(k))

    def step_back_core(k):
        arrive(from_core(k))
        for family in (to_core, to_shard, to_side, to_deep, from_deep, from_side, from_core):
            for one in family(k):
                one.wait_send()

    steps = (
        step_start,
        step_core,
        step_shard,
        step_side,
        step_deep,
        step_back_deep,
        step_back_side,
        step_back_core,
    )

    def tick(t, carry):
        for lag, step in enumerate(steps):
            k = t - lag

            @pl.when((k >= 0) & (k < chunks))
            def _(step=step, k=k):
                step(k)

        return carry

    lax.fori_loop(0, chunks + len(steps) - 1, tick, 0)


def sum_grads(matrices, gains, shards, replicas, identity):
    blocks = [
        matrix.astype(jnp.bfloat16).reshape(shards, matrix.shape[0] // shards, -1)
        for matrix in matrices
    ]
    if gains:
        line = jnp.concatenate([g.astype(jnp.bfloat16).reshape(shards, 1, -1) for g in gains], 2)
        blocks.append(jnp.pad(line, ((0, 0), (0, UNIT - 1), (0, PACK - line.shape[2]))))
    pieces = [block.shape[1] for block in blocks for _ in range(0, block.shape[2], PACK)]
    rows = UNIT * replicas
    chunks = -(-sum(pieces) // rows)
    depth = replicas // 4
    slots = shards + 2 * depth + 1
    kind = jnp.bfloat16
    count = len(blocks)
    total = pl.pallas_call(
        functools.partial(reduce_kernel, shards, depth, chunks, rows, count),
        out_shape=jax.ShapeDtypeStruct((chunks * rows, PACK), kind),
        in_specs=[pl.BlockSpec(memory_space=pl.ANY)] * count,
        out_specs=pl.BlockSpec(memory_space=pltpu.VMEM),
        scratch_shapes=[
            pltpu.VMEM((shards, chunks * rows, PACK), kind),
            pltpu.VMEM((chunks, shards, rows // 2, PACK), kind),
            pltpu.VMEM((chunks, shards - 1, rows // 2, PACK), kind),
            pltpu.VMEM((chunks, rows // 4, PACK), kind),
            pltpu.VMEM((chunks, depth - 1, UNIT, PACK), kind),
            pltpu.SemaphoreType.DMA((len(pieces),)),
            pltpu.SemaphoreType.DMA((chunks, slots)),
            pltpu.SemaphoreType.DMA((chunks, slots)),
        ],
        compiler_params=pltpu.CompilerParams(
            collective_id=identity, has_side_effects=True, vmem_limit_bytes=48 * 1024 * 1024
        ),
        name="reduce_terms",
    )(*blocks)
    results, start = [], 0
    for matrix in matrices:
        size = matrix.shape[0] // shards
        parts = []
        for _ in range(0, matrix.shape[1], PACK):
            parts.append(total[start : start + size].astype(jnp.float32))
            start += size
        results.append(jnp.concatenate(parts, 1))
    for i, gain in enumerate(gains):
        size = gain.shape[0] // shards
        results.append(total[start, i * size : (i + 1) * size].astype(jnp.float32))
    return results


def on_device(
    tokens,
    cotangent,
    positions,
    rest,
    first_gain,
    second_gain,
    merged_weight,
    output_weight,
    input_weight,
    down_weight,
):
    shards = lax.axis_size("shard")
    replicas = lax.axis_size("replica")
    gain_size = first_gain.shape[0]
    gains = jnp.concatenate([first_gain, second_gain])[None, :]
    gains = jnp.pad(gains, ((0, UNIT - 1), (0, -gains.shape[1] % 128)))
    fulls = gather_weights(
        [gains, merged_weight, output_weight, input_weight, down_weight], shards
    )
    gain_one = fulls[0][:, 0, :gain_size].reshape(-1)
    gain_two = fulls[0][:, 0, gain_size : 2 * gain_size].reshape(-1)
    merged_full, output_full, input_full, down_full = [
        full.reshape(-1, full.shape[2]) for full in fulls[1:]
    ]
    rows = tokens.shape[0]
    place = lax.axis_index(("replica", "shard"))
    count = lax.axis_size(("replica", "shard"))
    scale = HEAD_DIM ** (-0.5)
    tokens_f = tokens.astype(jnp.float32)
    norm_one, pull_one = jax.vjp(layer_norm, tokens_f, gain_one.astype(jnp.float32))
    norm_one_low = norm_one.astype(jnp.bfloat16)
    merged = jnp.dot(norm_one_low, merged_full, preferred_element_type=jnp.float32)
    cosine, sine = rotary_tables(positions)
    query = rotate(merged[:, :D].reshape(rows, HEADS, HEAD_DIM), cosine, sine).astype(jnp.bfloat16)
    keys = rotate(merged[:, D : 2 * D].reshape(rows, HEADS, HEAD_DIM), cosine, sine).astype(
        jnp.bfloat16
    )
    values = merged[:, 2 * D :].astype(jnp.bfloat16)
    pairs = jnp.concatenate([keys.reshape(rows, D), values], 1)
    pairs_wide = extended(pairs, ((("replica", "shard"), 0),), WINDOW)
    keys_wide = pairs_wide[:, :D].reshape(-1, HEADS, HEAD_DIM)
    values_wide = pairs_wide[:, D:].reshape(-1, HEADS, HEAD_DIM)
    allowed = window_mask(positions, rest, rows, place, count)[None]
    scores = (
        jnp.einsum("qhd,khd->hqk", query, keys_wide, preferred_element_type=jnp.float32) * scale
    )
    scores = jnp.where(allowed, scores, NEGATIVE)
    peak = jnp.max(scores, -1, keepdims=True)
    expo = jnp.exp(scores - peak)
    total = jnp.sum(expo, -1, keepdims=True)
    log_total = peak + jnp.log(total)
    prob = expo / total
    context = jnp.einsum(
        "hqk,khd->qhd", prob.astype(jnp.bfloat16), values_wide, preferred_element_type=jnp.float32
    )
    context = context.reshape(rows, D).astype(jnp.bfloat16)
    resid = tokens_f + jnp.dot(context, output_full, preferred_element_type=jnp.float32)
    norm_two, pull_two = jax.vjp(layer_norm, resid, gain_two.astype(jnp.float32))
    norm_two_low = norm_two.astype(jnp.bfloat16)
    hidden = jnp.dot(norm_two_low, input_full, preferred_element_type=jnp.float32)
    act, pull_act = jax.vjp(gated, hidden[:, :FF], hidden[:, FF:])
    act_low = act.astype(jnp.bfloat16)
    mixed = (resid + jnp.dot(act_low, down_full, preferred_element_type=jnp.float32)).astype(
        jnp.bfloat16
    )
    down_grad = jnp.einsum("tf,td->fd", act_low, cotangent, preferred_element_type=jnp.float32)
    grad_act = jnp.einsum("td,fd->tf", cotangent, down_full, preferred_element_type=jnp.float32)
    grad_gate, grad_up = pull_act(grad_act)
    grad_hidden = jnp.concatenate([grad_gate, grad_up], 1).astype(jnp.bfloat16)
    input_grad = jnp.einsum(
        "td,tf->df", norm_two_low, grad_hidden, preferred_element_type=jnp.float32
    )
    grad_norm_two = jnp.einsum(
        "tf,df->td", grad_hidden, input_full, preferred_element_type=jnp.float32
    )
    grad_resid_norm, second_gain_grad = pull_two(grad_norm_two)
    grad_resid = cotangent.astype(jnp.float32) + grad_resid_norm
    grad_resid_low = grad_resid.astype(jnp.bfloat16)
    output_grad = jnp.einsum(
        "td,te->de", context, grad_resid_low, preferred_element_type=jnp.float32
    )
    grad_context = jnp.einsum(
        "te,de->td", grad_resid_low, output_full, preferred_element_type=jnp.float32
    )
    grad_context = grad_context.astype(jnp.bfloat16).reshape(rows, HEADS, HEAD_DIM)
    scores_again = (
        jnp.einsum("qhd,khd->hqk", query, keys_wide, preferred_element_type=jnp.float32) * scale
    )
    scores_again = jnp.where(allowed, scores_again, NEGATIVE)
    prob_again = jnp.exp(scores_again - log_total)
    value_grad = jnp.einsum(
        "hqk,qhd->khd",
        prob_again.astype(jnp.bfloat16),
        grad_context,
        preferred_element_type=jnp.float32,
    )
    grad_prob = jnp.einsum(
        "qhd,khd->hqk", grad_context, values_wide, preferred_element_type=jnp.float32
    )
    grad_scores = prob_again * (grad_prob - jnp.sum(prob_again * grad_prob, -1, keepdims=True))
    grad_scores = grad_scores.astype(jnp.bfloat16)
    query_grad = (
        jnp.einsum("hqk,khd->qhd", grad_scores, keys_wide, preferred_element_type=jnp.float32)
        * scale
    )
    key_grad = (
        jnp.einsum("hqk,qhd->khd", grad_scores, query, preferred_element_type=jnp.float32) * scale
    )
    pair_grads = jnp.concatenate([key_grad.reshape(-1, D), value_grad.reshape(-1, D)], 1)
    middle = jnp.zeros((rows - 2 * WINDOW, 2 * D), jnp.float32)
    rims = jnp.concatenate([pair_grads[:WINDOW], middle, pair_grads[rows + WINDOW :]], 0)
    arrived = extended(rims.astype(jnp.bfloat16), ((("replica", "shard"), 0),), WINDOW).astype(
        rims.dtype
    )
    pair_own = pair_grads[WINDOW : rows + WINDOW] + jnp.concatenate(
        [arrived[:WINDOW], middle, arrived[rows + WINDOW :]], 0
    )
    grad_merged = jnp.concatenate(
        [
            unrotate(query_grad, cosine, sine).reshape(rows, D),
            unrotate(pair_own[:, :D].reshape(rows, HEADS, HEAD_DIM), cosine, sine).reshape(rows, D),
            pair_own[:, D:],
        ],
        1,
    ).astype(jnp.bfloat16)
    merged_grad = jnp.einsum(
        "td,te->de", norm_one_low, grad_merged, preferred_element_type=jnp.float32
    )
    grad_norm_one = jnp.einsum(
        "te,de->td", grad_merged, merged_full, preferred_element_type=jnp.float32
    )
    grad_tokens_norm, first_gain_grad = pull_one(grad_norm_one)
    token_grad = grad_resid + grad_tokens_norm
    merged_sum, output_sum, input_sum, down_sum, first_sum, second_sum = sum_grads(
        [merged_grad, output_grad, input_grad, down_grad],
        [first_gain_grad, second_gain_grad],
        shards,
        replicas,
        1,
    )
    return (
        mixed,
        token_grad,
        first_sum,
        second_sum,
        merged_sum,
        output_sum,
        input_sum,
        down_sum,
    )


def solution(mesh):
    return jax.shard_map(
        on_device,
        mesh=mesh,
        in_specs=(
            P(("replica", "shard"), None),
            P(("replica", "shard"), None),
            P(("replica", "shard")),
            P(("replica", "shard")),
            P("shard"),
            P("shard"),
            P("shard", None),
            P("shard", None),
            P("shard", None),
            P("shard", None),
        ),
        out_specs=(
            P(("replica", "shard"), None),
            P(("replica", "shard"), None),
            P("shard"),
            P("shard"),
            P("shard", None),
            P("shard", None),
            P("shard", None),
            P("shard", None),
        ),
        check_vma=False,
    )
```
